512 devices in a mesh: mem: 64 (over x_hi, z, core), hist: 8 (over y, x_lo).
Axes of the slice: x: 4 (x_hi: 2, x_lo: 2; x = x_hi * 2 + x_lo), y: 4, z: 16, core: 2. Of those that a mesh axis runs over, the one named last changes fastest.
Arguments:
- memory_block: bfloat16 [256, 64, 64, 128], P('mem', 'hist'), may hold values from -1.5 to 1.5
- memory_rows: bfloat16 [131072, 2, 128], P(('mem', 'hist')), may hold values from -6 to 6
- panel_rows: bfloat16 [32768, 2, 128], P(('hist', 'mem')), may hold values from -6 to 6
- time_deal: int32 [256], replicated, may hold values from 0 to 255, each once
- column_times: int32 [64], replicated, may hold values from 0 to 255
- window_start: int32 [1], replicated, may hold values from 0 to 128
- coupling: float32 [64, 64], replicated, may hold values from -0.375 to 0.375
- hamiltonian: bfloat16 [64, 64], replicated, may hold values from -6 to 6
Outputs:
- new_rows: bfloat16 [32768, 2, 128], P(('hist', 'mem'))
- new_sigma: bfloat16 [32768, 2, 128], P(('hist', 'mem'))
The draws below stay inside these ranges and needn't reach their ends.
Inputs may be any that keep to these rules, and one draw needn't show every extreme that they name: `time_deal`: each of 0 to 255 once.
All inputs are finite; a program needn't handle non-finite values.
Results may differ from the reference program's by a relative error of at most 0.014.
Values may be sent and summed in bfloat16 or wider, within the bound.
A program may use at most 64 MiB of HBM per device.

```python
import jax
import jax.numpy as jnp
from jax import lax

NO = 64
P_SIZE = 8
NPAN = 2
W = 256
C = 64


def place_ends(array, key, smallest, top_value):
    longest = array.shape.index(max(array.shape))
    spots = []
    for shift in (0, 1):
        where = [jax.random.randint(jax.random.fold_in(key, axis), (), 0, length) for axis, length in enumerate(array.shape)]
        where[longest] = (where[longest] + shift) % array.shape[longest]
        spots.append(tuple(where))
    return array.at[spots[0]].set(smallest).at[spots[1]].set(top_value)


def steps_of(stream_key, dims, split, smallest, top_value):
    level, own = 1.0, jax.random.fold_in(stream_key, 6)
    for axis_at, blocks in split:
        draws = jnp.exp(jax.random.uniform(jax.random.fold_in(own, axis_at), (blocks,), jnp.float32, smallest / len(split), top_value / len(split)))
        level = level * jnp.repeat(draws, dims[axis_at] // blocks).reshape([-1 if axis == axis_at else 1 for axis in range(len(dims))])
    return level


def centred(rng, extent, scale, most, pieces=(), kind=jnp.bfloat16):
    loudness = steps_of(rng, extent, pieces, -0.22, 0.18) if pieces else 1.0
    result = jax.random.normal(rng, extent, jnp.float32) * scale * loudness
    return jnp.minimum(jnp.maximum(result, -most), most).astype(kind)


def setup_inputs(seed: int = 0) -> dict:
    keys = jax.random.split(jax.random.key(seed), 9)
    memory_block = centred(keys[0], (W, C, NO, 2 * NO), 0.25, 1.5, ((0, 64), (1, 8)))
    memory_rows = centred(keys[1], (W * P_SIZE * NO, NPAN, 2 * NO), 1.0, 6.0, ((0, 512),))
    panel_rows = centred(keys[2], (C * P_SIZE * NO, NPAN, 2 * NO), 1.0, 6.0, ((0, 512),))
    time_deal = jax.random.permutation(keys[3], W).astype(jnp.int32)
    column_times = place_ends(jax.random.randint(keys[4], (C,), 0, W), jax.random.fold_in(keys[4], 1), 0, W - 1).astype(jnp.int32)
    window_start = jax.random.randint(keys[5], (1,), 0, W // 2 + 1).astype(jnp.int32)
    coupling = centred(keys[6], (NO, NO), (4 * NO) ** -0.5, 0.375, (), jnp.float32)
    hamiltonian = centred(keys[7], (NO, NO), 1.0, 6.0)
    return dict(memory_block=memory_block, memory_rows=memory_rows, panel_rows=panel_rows, time_deal=time_deal, column_times=column_times, window_start=window_start, coupling=coupling, hamiltonian=hamiltonian)


time_step = 0.02


def sigma_of(tiles, coupling):
    orbitals = coupling.shape[0]
    real_part = tiles[..., :orbitals]
    imag_part = tiles[..., orbitals:]
    bubble = real_part * real_part + imag_part * imag_part
    screened = jnp.einsum('ik,...kpl->...ipl', coupling, bubble, precision=lax.Precision.HIGHEST)
    screening = jnp.einsum('...ipl,jl->...ipj', screened, coupling, precision=lax.Precision.HIGHEST)
    return -jnp.concatenate([real_part * screening, imag_part * screening], -1)


def complex_form(tiles):
    orbitals = tiles.shape[-1] // 2
    real_part = tiles[..., :orbitals]
    imag_part = tiles[..., orbitals:]
    upper = jnp.concatenate([real_part, imag_part], -1)
    lower = jnp.concatenate([-imag_part, real_part], -1)
    return jnp.concatenate([upper, lower], -2)


def reference(memory_block, memory_rows, panel_rows, time_deal, column_times, window_start, coupling, hamiltonian):
    memory_tiles = memory_rows.reshape(W, P_SIZE, NO, NPAN, 2 * NO).astype(jnp.float32)
    old_sigma = sigma_of(memory_tiles, coupling).astype(jnp.bfloat16).astype(jnp.float32)
    causal = (time_deal[:, None] >= column_times[None, :]) & (time_deal[:, None] >= window_start[0])

    def column_term(operands):
        column_tiles, column_mask = operands
        block_form = complex_form(column_tiles.astype(jnp.float32)) * column_mask[:, None, None].astype(jnp.float32)
        return jnp.einsum('ktipr,krc->tipc', old_sigma, block_form)

    collision = lax.map(column_term, (jnp.swapaxes(memory_block, 0, 1), causal.T))
    panel_tiles = panel_rows.reshape(C, P_SIZE, NO, NPAN, 2 * NO).astype(jnp.float32)
    applied = jnp.einsum('ik,jtkpc->jtipc', hamiltonian.astype(jnp.float32), panel_tiles)
    turned = jnp.concatenate([applied[..., NO:], -applied[..., :NO]], -1)
    advanced = (panel_tiles + time_step * (turned + collision)).astype(jnp.bfloat16)
    new_sigma = sigma_of(advanced.astype(jnp.float32), coupling).astype(jnp.bfloat16)
    return advanced.reshape(C * P_SIZE * NO, NPAN, 2 * NO), new_sigma.reshape(C * P_SIZE * NO, NPAN, 2 * NO)
```

```python
import jax
import jax.numpy as jnp
from jax import lax
from jax.experimental import pallas as pl
from jax.experimental.pallas import tpu as pltpu
from jax.sharding import PartitionSpec as P


MESH = pl.DeviceIdType.MESH
BF16 = jnp.bfloat16
F32 = jnp.float32
P_SIZE = 8
TIME_STEP = 0.02
NZ = 16
NY = 4
HALF = NZ // 2


def halves(x):
    high = x.astype(BF16)
    return high, (x - high.astype(F32)).astype(BF16)


def dot(a, b):
    return jnp.dot(a, b, preferred_element_type=F32)


def chosen(shape, test):
    rows = lax.broadcasted_iota(jnp.int32, shape, 0)
    columns = lax.broadcasted_iota(jnp.int32, shape, 1)
    return jnp.where(test(rows, columns), 1.0, 0.0).astype(BF16)


def pair_form(small):
    spread = chosen((128, 64), lambda r, c: (r >> 1) == c)
    gather = chosen((64, 128), lambda r, c: r == (c >> 1))
    wide = dot(dot(spread, small).astype(BF16), gather)
    same = chosen((128, 128), lambda r, c: (r & 1) == (c & 1))
    return wide.astype(BF16) * same


def lane_form(small):
    spread = chosen((128, 64), lambda r, c: (r & 63) == c)
    gather = chosen((64, 128), lambda r, c: r == (c & 63))
    turned = lax.dot_general(spread, small, (((1,), (1,)), ((), ())), preferred_element_type=F32)
    return dot(turned.astype(BF16), gather).astype(BF16)


def sigma_of(x, left, right):
    count = x.shape[0] // 128
    wide = x.astype(F32)
    high, low = halves(wide * wide)
    over = dot(jnp.concatenate([high, low, high], axis=1), right)
    high, low = halves(over)
    result = []
    for n in range(count):
        rows = slice(n * 128, (n + 1) * 128)
        stacked = jnp.concatenate([high[rows], low[rows], high[rows]], axis=0)
        result.append(-(wide[rows] * dot(left, stacked)))
    return result


def kernel(
    time_deal, column_times, window_start, block_ref, memory_ref, panel_ref, coupling_ref, hamiltonian_ref,
    rows_ref, sigma_ref,
    blocks, forms, own_sigma, old_sigma, partial, up_in, up_out, down_in, down_out, last_in, cross_out,
    block_sem, core_sem, y_sem, x_sem, y2_sem, xy_sem, x2_sem,
    up_sem, down_sem, last_sem, cross_sem,
    block_send, core_send, y_send, x_send, y2_send, xy_send, x2_send, up_send, down_send,
):
    mem = lax.axis_index("mem")
    hist = lax.axis_index("hist")
    core = lax.rem(mem, 2)
    z = lax.rem(lax.div(mem, 2), NZ)
    x_hi = lax.div(mem, 2 * NZ)
    y = lax.div(hist, 2)
    x_lo = lax.rem(hist, 2)
    chip = mem - core
    y_next = (lax.rem(y + 1, NY), lax.rem(y + NY - 1, NY))
    y_far = lax.rem(y + 2, NY)
    z_next = (lax.rem(z + 1, NZ), lax.rem(z + NZ - 1, NZ))

    def at_mem(xx, zz):
        return xx * (2 * NZ) + zz * 2 + core

    def at_hist(yy, xx):
        return yy * 2 + xx

    def send(src, dst, send_sem, recv_sem, where):
        copy = pltpu.make_async_remote_copy(
            src_ref=src, dst_ref=dst, send_sem=send_sem, recv_sem=recv_sem, device_id=where, device_id_type=MESH
        )
        return copy

    other_x = at_hist(y, 1 - x_lo)
    peers = [(chip + 1 - core, hist)]
    peers += [(chip + q, other_x) for q in range(2)]
    peers += [(chip + q, at_hist(yy, x_lo)) for yy in y_next for q in range(2)]
    peers += [(at_mem(xx, zz), hist) for xx in range(2) for zz in z_next]
    peers += [(at_mem(1 - x_hi, z), hist)]
    barrier = pltpu.get_barrier_semaphore()
    for peer in peers:
        pl.semaphore_signal(barrier, inc=1, device_id=peer, device_id_type=MESH)

    block_here = pltpu.make_async_copy(block_ref, blocks.at[core], block_send.at[0])
    block_here.start()

    coupling_high, coupling_low = halves(coupling_ref[...])
    left_high, left_low = pair_form(coupling_high), pair_form(coupling_low)
    left = jnp.concatenate([left_high, left_high, left_low], axis=1)
    right_high, right_low = lane_form(coupling_high), lane_form(coupling_low)
    right = jnp.concatenate([right_high, right_high, right_low], axis=0)
    for u, tile in enumerate(sigma_of(memory_ref[...], left, right)):
        own_sigma[u % 2, u // 2] = tile.astype(BF16)

    pl.semaphore_wait(barrier, len(peers))

    mine = core * NY + y
    first = []
    first.append(send(own_sigma.at[1 - core], old_sigma.at[x_lo, mine], core_send, core_sem, (chip + 1 - core, hist)))
    for q in range(2):
        for d in range(2):
            first.append(
                send(own_sigma.at[q], old_sigma.at[x_lo, mine], y_send.at[d, q], y_sem.at[d, core],
                     (chip + q, at_hist(y_next[d], x_lo)))
            )
        first.append(send(own_sigma.at[q], old_sigma.at[x_lo, mine], x_send.at[q], x_sem.at[core], (chip + q, other_x)))
    block_there = send(block_ref, blocks.at[core], block_send.at[1], block_sem, (chip + 1 - core, hist))
    for copy in first:
        copy.start()
    block_there.start()
    old_sigma[x_lo, mine] = own_sigma[core]

    def arrived(dst, sem):
        send(dst, dst, sem, sem, peers[0]).wait_recv()

    sign = jnp.where(lax.broadcasted_iota(jnp.int32, (64, 128), 1) < 64, -1.0, 1.0)
    start = window_start[0]

    def build(which):
        for k in range(4):
            slot_time = time_deal[(chip + which) * 4 + k]
            for j in range(8):
                keep = (slot_time >= column_times[hist * 8 + j]) & (slot_time >= start)
                level = jnp.where(keep, 1.0, 0.0)
                tile = blocks[which, k, j].astype(F32) * level
                row = pl.multiple_of((which * 4 + k) * 128, 128)
                forms[pl.ds(row, 64), j * 128 : (j + 1) * 128] = tile.astype(BF16)
                forms[pl.ds(row + 64, 64), j * 128 : (j + 1) * 128] = (pltpu.roll(tile, 64, 1) * sign).astype(BF16)

    block_here.wait()
    build(core)

    panel = panel_ref[...]
    applied = dot(pair_form(hamiltonian_ref[...]), panel)
    turned = pltpu.roll(applied, 64, 1) * jnp.where(lax.broadcasted_iota(jnp.int32, (128, 128), 1) < 64, 1.0, -1.0)
    base = panel.astype(F32) + TIME_STEP * turned

    block_there.wait_recv()
    build(1 - core)

    second = []
    for q in range(2):
        for d in range(2):
            kk = q * NY + y_next[1 - d]
            arrived(old_sigma.at[x_lo, kk], y_sem.at[d, q])
            copy = send(old_sigma.at[x_lo, kk, d], old_sigma.at[x_lo, kk, d], y2_send.at[d, q], y2_sem.at[d, q],
                        (mem, at_hist(y_next[d], x_lo)))
            copy.start()
            second.append(copy)
    for q in range(2):
        kk = q * NY + y
        arrived(old_sigma.at[1 - x_lo, kk], x_sem.at[q])
        for d in range(2):
            copy = send(old_sigma.at[1 - x_lo, kk], old_sigma.at[1 - x_lo, kk], xy_send.at[d, q], xy_sem.at[d, q],
                        (mem, at_hist(y_next[d], x_lo)))
            copy.start()
            second.append(copy)
    for q in range(2):
        for d in range(2):
            kk = q * NY + y_far
            arrived(old_sigma.at[x_lo, kk, d], y2_sem.at[d, q])
            copy = send(old_sigma.at[x_lo, kk, d], old_sigma.at[x_lo, kk, d], x2_send.at[d, q], x2_sem.at[d, q],
                        (mem, other_x))
            copy.start()
            second.append(copy)
    arrived(old_sigma.at[x_lo, (1 - core) * NY + y], core_sem)

    def multiply(xx):
        lhs = jnp.concatenate(
            [jnp.concatenate([old_sigma[xx, kk, u] for kk in range(8)], axis=1) for u in range(2)], axis=0
        )
        for j in range(4):
            columns = slice(j * 256, (j + 1) * 256)
            product = dot(lhs, forms[:, columns])
            for u in range(2):
                for i in range(2):
                    partial[xx * 2 + u, 2 * j + i] = product[u * 128 : (u + 1) * 128, i * 128 : (i + 1) * 128]

    multiply(x_lo)
    for q in range(2):
        for d in range(2):
            arrived(old_sigma.at[1 - x_lo, q * NY + y_next[1 - d]], xy_sem.at[d, q])
    for q in range(2):
        for d in range(2):
            arrived(old_sigma.at[1 - x_lo, q * NY + y_far, d], x2_sem.at[d, q])
    multiply(1 - x_lo)

    def term(zz, xx):
        return partial[lax.rem(zz, 4), 4 * xx + lax.div(zz, 4)]

    third = []
    cross_out[...] = term(z, 1 - x_hi).astype(BF16)
    copy = send(cross_out, last_in.at[4], cross_sem, last_sem.at[4], (at_mem(1 - x_hi, z), hist))
    copy.start()
    third.append(copy)
    for s in range(HALF):
        for b in range(2):
            for d, steps, came, went, in_sem, out_sem in (
                (0, HALF, up_in, up_out, up_sem, up_send),
                (1, HALF - 1, down_in, down_out, down_sem, down_send),
            ):
                if s >= steps:
                    continue
                far = lax.rem(z + HALF - s, NZ) if d == 0 else lax.rem(z + NZ - (HALF - 1) + s, NZ)
                value = term(far, b)
                if s > 0:
                    arrived(came.at[s - 1, b], in_sem.at[s - 1, b])
                    value = value + came[s - 1, b].astype(F32)
                went[s, b] = value.astype(BF16)
                if s < steps - 1:
                    copy = send(went.at[s, b], came.at[s, b], out_sem.at[s, b], in_sem.at[s, b],
                                (at_mem(x_hi, z_next[d]), hist))
                else:
                    copy = send(went.at[s, b], last_in.at[d * 2 + x_hi], out_sem.at[s, b], last_sem.at[d * 2 + x_hi],
                                (at_mem(b, z_next[d]), hist))
                copy.start()
                third.append(copy)

    total = term(z, x_hi)
    for n in (4, 2, 3, 0, 1):
        arrived(last_in.at[n], last_sem.at[n])
        total = total + last_in[n].astype(F32)
    advanced = (base + TIME_STEP * total).astype(BF16)
    rows_ref[...] = advanced
    [new_sigma] = sigma_of(advanced, left, right)
    sigma_ref[...] = new_sigma.astype(BF16)

    for copy in first + [block_there] + second + third:
        copy.wait_send()


def local(memory_block, memory_rows, panel_rows, time_deal, column_times, window_start, coupling, hamiltonian):
    tile = (128, 128)
    dma = pltpu.SemaphoreType.DMA
    vmem = pl.BlockSpec(memory_space=pltpu.VMEM)
    smem = pl.BlockSpec(memory_space=pltpu.SMEM)
    new_rows, new_sigma = pl.pallas_call(
        kernel,
        out_shape=[jax.ShapeDtypeStruct(tile, BF16)] * 2,
        in_specs=[smem, smem, smem, pl.BlockSpec(memory_space=pl.ANY), vmem, vmem, vmem, vmem],
        out_specs=[vmem, vmem],
        scratch_shapes=[
            pltpu.VMEM((2, 4, 8, 64, 128), BF16),
            pltpu.VMEM((1024, 1024), BF16),
            pltpu.VMEM((2, 2, *tile), BF16),
            pltpu.VMEM((2, 8, 2, *tile), BF16),
            pltpu.VMEM((4, 8, *tile), F32),
            pltpu.VMEM((HALF - 1, 2, *tile), BF16),
            pltpu.VMEM((HALF, 2, *tile), BF16),
            pltpu.VMEM((HALF - 2, 2, *tile), BF16),
            pltpu.VMEM((HALF - 1, 2, *tile), BF16),
            pltpu.VMEM((5, *tile), BF16),
            pltpu.VMEM(tile, BF16),
            dma, dma, dma((2, 2)), dma((2,)), dma((2, 2)), dma((2, 2)), dma((2, 2)),
            dma((HALF - 1, 2)), dma((HALF - 2, 2)), dma((5,)), dma,
            dma((2,)), dma, dma((2, 2)), dma((2,)), dma((2, 2)), dma((2, 2)), dma((2, 2)),
            dma((HALF, 2)), dma((HALF - 1, 2)),
        ],
        compiler_params=pltpu.CompilerParams(
            collective_id=0, has_side_effects=True, vmem_limit_bytes=32 * 2**20
        ),
        cost_estimate=pl.CostEstimate(flops=1100000000, bytes_accessed=2000000, transcendentals=0),
    )(
        time_deal, column_times, window_start, memory_block,
        memory_rows.reshape(512, 128), panel_rows.reshape(128, 128), coupling, hamiltonian,
    )
    return new_rows.reshape(panel_rows.shape), new_sigma.reshape(panel_rows.shape)


def solution(mesh):
    in_specs = (
        P("mem", "hist", None, None),
        P(("mem", "hist"), None, None),
        P(("hist", "mem"), None, None),
        P(),
        P(),
        P(),
        P(),
        P(),
    )
    out_specs = (P(("hist", "mem"), None, None), P(("hist", "mem"), None, None))
    return jax.shard_map(local, mesh=mesh, in_specs=in_specs, out_specs=out_specs, check_vma=False)
```

```python
import jax
import jax.numpy as jnp
from jax import lax
from jax.experimental import pallas as pl
from jax.experimental.pallas import tpu as pltpu
from jax.sharding import PartitionSpec as P


MESH = pl.DeviceIdType.MESH
BF16 = jnp.bfloat16
F32 = jnp.float32
P_SIZE = 8
TIME_STEP = 0.02
NZ = 16
NY = 4
HALF = NZ // 2
ORDER = (0, 3, 1, 2)


def halves(x):
    high = x.astype(BF16)
    return high, (x - high.astype(F32)).astype(BF16)


def dot(a, b):
    return jnp.dot(a, b, preferred_element_type=F32)


def chosen(shape, test):
    rows = lax.broadcasted_iota(jnp.int32, shape, 0)
    columns = lax.broadcasted_iota(jnp.int32, shape, 1)
    return jnp.where(test(rows, columns), 1.0, 0.0).astype(BF16)


def pair_form(small):
    spread = chosen((128, 64), lambda r, c: (r >> 1) == c)
    gather = chosen((64, 128), lambda r, c: r == (c >> 1))
    wide = dot(dot(spread, small).astype(BF16), gather)
    same = chosen((128, 128), lambda r, c: (r & 1) == (c & 1))
    return wide.astype(BF16) * same


def lane_form(small):
    spread = chosen((128, 64), lambda r, c: (r & 63) == c)
    gather = chosen((64, 128), lambda r, c: r == (c & 63))
    turned = lax.dot_general(spread, small, (((1,), (1,)), ((), ())), preferred_element_type=F32)
    return dot(turned.astype(BF16), gather).astype(BF16)


def sigma_of(x, left, right):
    count = x.shape[0] // 128
    wide = x.astype(F32)
    high, low = halves(wide * wide)
    over = dot(jnp.concatenate([high, low, high], axis=1), right)
    high, low = halves(over)
    result = []
    for n in range(count):
        rows = slice(n * 128, (n + 1) * 128)
        stacked = jnp.concatenate([high[rows], low[rows], high[rows]], axis=0)
        result.append(-(wide[rows] * dot(left, stacked)))
    return result


def kernel(
    time_hbm, column_hbm, window_hbm, block_ref, memory_hbm, panel_hbm, coupling_hbm, hamiltonian_hbm,
    rows_ref, sigma_ref,
    time_deal, column_times, window_start, memory_ref, panel_ref, coupling_ref, hamiltonian_ref,
    blocks, forms, own_sigma, old_sigma, partial, up_in, up_out, down_in, down_out, last_in, cross_out,
    load_sem, block_sem, block_send, tile_sem, first_send, pass_send,
    up_sem, down_sem, last_sem, cross_send, up_send, down_send,
):
    mem = lax.axis_index("mem")
    hist = lax.axis_index("hist")
    core = lax.rem(mem, 2)
    z = lax.rem(lax.div(mem, 2), NZ)
    x_hi = lax.div(mem, 2 * NZ)
    y = lax.div(hist, 2)
    x_lo = lax.rem(hist, 2)
    chip = mem - core
    y_next = (lax.rem(y + 1, NY), lax.rem(y + NY - 1, NY))
    y_far = lax.rem(y + 2, NY)
    z_next = (lax.rem(z + 1, NZ), lax.rem(z + NZ - 1, NZ))

    def at_mem(xx, zz):
        return xx * (2 * NZ) + zz * 2 + core

    def at_hist(yy, xx):
        return yy * 2 + xx

    def send(src, dst, send_sem, recv_sem, where):
        return pltpu.make_async_remote_copy(
            src_ref=src, dst_ref=dst, send_sem=send_sem, recv_sem=recv_sem, device_id=where, device_id_type=MESH
        )

    other_core = (chip + 1 - core, hist)
    other_x = at_hist(y, 1 - x_lo)
    peers = [other_core]
    peers += [(chip + q, other_x) for q in range(2)]
    peers += [(chip + q, at_hist(yy, x_lo)) for yy in (*y_next, y_far) for q in range(2)]
    peers += [(at_mem(xx, zz), hist) for xx in range(2) for zz in z_next]
    peers += [(at_mem(1 - x_hi, z), hist)]
    barrier = pltpu.get_barrier_semaphore()
    for peer in peers:
        pl.semaphore_signal(barrier, inc=1, device_id=peer, device_id_type=MESH)

    loads = [
        pltpu.make_async_copy(src, dst, load_sem.at[n])
        for n, (src, dst) in enumerate((
            (coupling_hbm, coupling_ref), (memory_hbm, memory_ref), (time_hbm, time_deal), (column_hbm, column_times),
            (window_hbm, window_start), (hamiltonian_hbm, hamiltonian_ref), (panel_hbm, panel_ref),
            (block_ref, blocks.at[core]),
        ))
    ]
    for copy in loads:
        copy.start()

    loads[0].wait()
    coupling_high, coupling_low = halves(coupling_ref[...])
    left_high, left_low = pair_form(coupling_high), pair_form(coupling_low)
    left = jnp.concatenate([left_high, left_high, left_low], axis=1)
    right_high, right_low = lane_form(coupling_high), lane_form(coupling_low)
    right = jnp.concatenate([right_high, right_high, right_low], axis=0)
    loads[1].wait()
    for u, tile in enumerate(sigma_of(memory_ref[...], left, right)):
        own_sigma[u % 2, u // 2] = tile.astype(BF16)

    pl.semaphore_wait(barrier, len(peers))

    mine = core * NY + y
    early = lax.div(lax.rem(2 * x_lo + 2 * NZ - z, 4), 2)
    first = []
    for n in range(2):
        u = early if n == 0 else 1 - early
        here = old_sigma.at[2 * x_lo + u, mine]
        arrival = tile_sem.at[2 * x_lo + u, mine]
        targets = []
        for yy in (y_far, *y_next):
            targets += [(q, (chip + q, at_hist(yy, x_lo))) for q in range(2)]
        targets += [(q, (chip + q, other_x)) for q in range(2)]
        targets += [(1 - core, other_core)]
        for i, (q, where) in enumerate(targets):
            copy = send(own_sigma.at[q, u], here, first_send.at[n, i], arrival, where)
            copy.start()
            first.append(copy)
        pltpu.make_async_copy(own_sigma.at[core, u], here, arrival).start()
    block_there = send(block_ref, blocks.at[core], block_send, block_sem, other_core)
    block_there.start()

    def arrived(dst, sem):
        send(dst, dst, sem, sem, other_core).wait_recv()

    sign = jnp.where(lax.broadcasted_iota(jnp.int32, (64, 128), 1) < 64, -1.0, 1.0)
    for n in (2, 3, 4):
        loads[n].wait()
    start = window_start[0]

    def build(which):
        for k in range(4):
            slot_time = time_deal[(chip + which) * 4 + k]
            for j in range(8):
                keep = (slot_time >= column_times[hist * 8 + j]) & (slot_time >= start)
                level = jnp.where(keep, 1.0, 0.0)
                tile = blocks[which, k, j].astype(F32) * level
                row = pl.multiple_of((which * 4 + k) * 128, 128)
                forms[pl.ds(row, 64), j * 128 : (j + 1) * 128] = tile.astype(BF16)
                forms[pl.ds(row + 64, 64), j * 128 : (j + 1) * 128] = (pltpu.roll(tile, 64, 1) * sign).astype(BF16)

    loads[7].wait()
    build(core)

    loads[5].wait()
    loads[6].wait()
    panel = panel_ref[...]
    applied = dot(pair_form(hamiltonian_ref[...]), panel)
    turned = pltpu.roll(applied, 64, 1) * jnp.where(lax.broadcasted_iota(jnp.int32, (128, 128), 1) < 64, 1.0, -1.0)
    base = panel.astype(F32) + TIME_STEP * turned

    def time_of(n):
        return lax.rem(z + ORDER[n], 4)

    def tile_in(t, kk):
        arrived(old_sigma.at[t, kk], tile_sem.at[t, kk])

    def pass_on(n):
        t = time_of(n)
        inside = lax.div(t, 2) == x_lo

        @pl.when(inside)
        def _():
            for q in range(2):
                kk = q * NY + y_far
                tile_in(t, kk)
                send(old_sigma.at[t, kk], old_sigma.at[t, kk], pass_send.at[t, q], tile_sem.at[t, kk], (mem, other_x)).start()

        @pl.when(jnp.logical_not(inside))
        def _():
            for q in range(2):
                kk = q * NY + y
                tile_in(t, kk)
                for d in range(2):
                    send(old_sigma.at[t, kk], old_sigma.at[t, kk], pass_send.at[t, 2 * q + d], tile_sem.at[t, kk],
                         (mem, at_hist(y_next[d], x_lo))).start()

    def complete(n):
        t = time_of(n)
        rest = jnp.where(lax.div(t, 2) == x_lo, y, y_far)
        for q in range(2):
            tile_in(t, q * NY + rest)
            for yy in y_next:
                tile_in(t, q * NY + yy)

    def multiply(n):
        t = time_of(n)
        lhs = jnp.concatenate([old_sigma[t, kk] for kk in range(8)], axis=1)
        for j in range(4):
            product = dot(lhs, forms[:, j * 256 : (j + 1) * 256])
            for i in range(2):
                partial[t, 2 * j + i] = product[:, i * 128 : (i + 1) * 128]

    def drain_passes(n):
        t = time_of(n)
        inside = lax.div(t, 2) == x_lo
        for i in range(2):
            send(old_sigma.at[t, i], old_sigma.at[t, i], pass_send.at[t, i], pass_send.at[t, i], other_core).wait_send()

        @pl.when(jnp.logical_not(inside))
        def _():
            for i in range(2, 4):
                send(old_sigma.at[t, i], old_sigma.at[t, i], pass_send.at[t, i], pass_send.at[t, i], other_core).wait_send()

    def term(zz, xx):
        return partial[lax.rem(zz, 4), 4 * xx + lax.div(zz, 4)]

    sent = {}

    def chain(d, s):
        came, went, in_sem, out_sem = ((up_in, up_out, up_sem, up_send), (down_in, down_out, down_sem, down_send))[d]
        far = lax.rem(z + HALF - s, NZ) if d == 0 else lax.rem(z + NZ - (HALF - 1) + s, NZ)
        for b in range(2):
            value = term(far, b)
            if s > 0:
                arrived(came.at[s - 1, b], in_sem.at[s - 1, b])
                value = value + came[s - 1, b].astype(F32)
            went[s, b] = value.astype(BF16)
            if s < HALF - 1 - d:
                dst, sem, where = came.at[s, b], in_sem.at[s, b], (at_mem(x_hi, z_next[d]), hist)
            else:
                dst, sem, where = last_in.at[d * 2 + x_hi], last_sem.at[d * 2 + x_hi], (at_mem(b, z_next[d]), hist)
            copy = send(went.at[s, b], dst, out_sem.at[s, b], sem, where)
            copy.start()
            sent[d, s, b] = copy

    def drain_chain(d, s):
        for b in range(2):
            sent[d, s, b].wait_send()

    pass_on(0)
    pass_on(1)
    block_there.wait_recv()
    build(1 - core)
    pass_on(2)
    complete(0)
    multiply(0)
    chain(0, 0)
    pass_on(3)
    complete(1)
    multiply(1)
    chain(0, 1)
    complete(2)
    multiply(2)
    chain(1, 0)
    complete(3)
    multiply(3)
    cross_out[...] = term(z, 1 - x_hi).astype(BF16)
    cross = send(cross_out, last_in.at[4], cross_send, last_sem.at[4], (at_mem(1 - x_hi, z), hist))
    chain(0, 2)
    chain(1, 1)
    cross.start()
    for copy in first:
        copy.wait_send()
    chain(0, 3)
    chain(1, 2)
    block_there.wait_send()
    for n in range(4):
        drain_passes(n)
    for s in range(4, HALF):
        chain(0, s)
        chain(1, s - 1)
        drain_chain(0, s - 4)
        drain_chain(1, s - 4)

    total = term(z, x_hi)
    for n in (4, 2, 3, 0, 1):
        arrived(last_in.at[n], last_sem.at[n])
        total = total + last_in[n].astype(F32)
    advanced = (base + TIME_STEP * total).astype(BF16)
    rows_ref[...] = advanced
    [new_sigma] = sigma_of(advanced, left, right)
    sigma_ref[...] = new_sigma.astype(BF16)

    cross.wait_send()
    for s in range(4, HALF):
        drain_chain(0, s)
        if s < HALF - 1:
            drain_chain(1, s)


def local(memory_block, memory_rows, panel_rows, time_deal, column_times, window_start, coupling, hamiltonian):
    tile = (128, 128)
    dma = pltpu.SemaphoreType.DMA
    vmem = pl.BlockSpec(memory_space=pltpu.VMEM)
    hbm = pl.BlockSpec(memory_space=pltpu.HBM)
    new_rows, new_sigma = pl.pallas_call(
        kernel,
        out_shape=[jax.ShapeDtypeStruct(tile, BF16)] * 2,
        in_specs=[hbm] * 8,
        out_specs=[vmem, vmem],
        scratch_shapes=[
            pltpu.SMEM(time_deal.shape, jnp.int32),
            pltpu.SMEM(column_times.shape, jnp.int32),
            pltpu.SMEM(window_start.shape, jnp.int32),
            pltpu.VMEM((512, 128), BF16),
            pltpu.VMEM(tile, BF16),
            pltpu.VMEM(coupling.shape, F32),
            pltpu.VMEM(hamiltonian.shape, BF16),
            pltpu.VMEM((2, 4, 8, 64, 128), BF16),
            pltpu.VMEM((1024, 1024), BF16),
            pltpu.VMEM((2, 2, *tile), BF16),
            pltpu.VMEM((4, 8, *tile), BF16),
            pltpu.VMEM((4, 8, *tile), F32),
            pltpu.VMEM((HALF - 1, 2, *tile), BF16),
            pltpu.VMEM((HALF, 2, *tile), BF16),
            pltpu.VMEM((HALF - 2, 2, *tile), BF16),
            pltpu.VMEM((HALF - 1, 2, *tile), BF16),
            pltpu.VMEM((5, *tile), BF16),
            pltpu.VMEM(tile, BF16),
            dma((8,)), dma, dma, dma((4, 8)), dma((2, 9)), dma((4, 4)),
            dma((HALF - 1, 2)), dma((HALF - 2, 2)), dma((5,)), dma, dma((HALF, 2)), dma((HALF - 1, 2)),
        ],
        compiler_params=pltpu.CompilerParams(
            collective_id=0, has_side_effects=True, vmem_limit_bytes=60 * 2**20
        ),
        cost_estimate=pl.CostEstimate(flops=1100000000, bytes_accessed=2000000, transcendentals=0),
    )(
        time_deal, column_times, window_start, memory_block,
        memory_rows.reshape(512, 128), panel_rows.reshape(128, 128), coupling, hamiltonian,
    )
    return new_rows.reshape(panel_rows.shape), new_sigma.reshape(panel_rows.shape)


def solution(mesh):
    in_specs = (
        P("mem", "hist", None, None),
        P(("mem", "hist"), None, None),
        P(("hist", "mem"), None, None),
        P(),
        P(),
        P(),
        P(),
        P(),
    )
    out_specs = (P(("hist", "mem"), None, None), P(("hist", "mem"), None, None))
    return jax.shard_map(local, mesh=mesh, in_specs=in_specs, out_specs=out_specs, check_vma=False)
```

```python
import jax
import jax.numpy as jnp
from jax import lax
from jax.experimental import pallas as pl
from jax.experimental.pallas import tpu as pltpu
from jax.sharding import PartitionSpec as P


MESH = pl.DeviceIdType.MESH
BF16 = jnp.bfloat16
F32 = jnp.float32
P_SIZE = 8
TIME_STEP = 0.02
NZ = 16
NY = 4
AHEAD, BEHIND = 8, 7
PARTS = (((7, 4), (3, 1)), ((8, 5), (4, 1)))
ORDER = (1, 0, 2, 3)


def halves(x):
    high = x.astype(BF16)
    return high, (x - high.astype(F32)).astype(BF16)


def dot(a, b):
    return jnp.dot(a, b, preferred_element_type=F32)


def chosen(shape, test):
    rows = lax.broadcasted_iota(jnp.int32, shape, 0)
    columns = lax.broadcasted_iota(jnp.int32, shape, 1)
    return jnp.where(test(rows, columns), 1.0, 0.0).astype(BF16)


def pair_form(small):
    spread = chosen((128, 64), lambda r, c: (r >> 1) == c)
    gather = chosen((64, 128), lambda r, c: r == (c >> 1))
    wide = dot(dot(spread, small).astype(BF16), gather)
    same = chosen((128, 128), lambda r, c: (r & 1) == (c & 1))
    return wide.astype(BF16) * same


def lane_form(small):
    spread = chosen((128, 64), lambda r, c: (r & 63) == c)
    gather = chosen((64, 128), lambda r, c: r == (c & 63))
    turned = lax.dot_general(spread, small, (((1,), (1,)), ((), ())), preferred_element_type=F32)
    return dot(turned.astype(BF16), gather).astype(BF16)


def sigma_of(x, left, right):
    count = x.shape[0] // 128
    wide = x.astype(F32)
    high, low = halves(wide * wide)
    over = dot(jnp.concatenate([high, low, high], axis=1), right)
    high, low = halves(over)
    result = []
    for n in range(count):
        rows = slice(n * 128, (n + 1) * 128)
        stacked = jnp.concatenate([high[rows], low[rows], high[rows]], axis=0)
        result.append(-(wide[rows] * dot(left, stacked)))
    return result


def kernel(
    time_hbm, column_hbm, window_hbm, block_ref, memory_hbm, panel_hbm, coupling_hbm, hamiltonian_hbm,
    both_ref,
    time_deal, column_times, window_start, memory_ref, panel_ref, coupling_ref, hamiltonian_ref,
    blocks, forms, own_sigma, old_sigma, partial, shared_out, shared_in, chain_in, chain_out, last_in, cross_out,
    load_sem, block_sem, block_send, tile_sem, first_send, pass_send,
    shared_send, shared_sem, chain_sem, chain_send, last_sem, cross_send,
):
    mem = lax.axis_index("mem")
    hist = lax.axis_index("hist")
    core = lax.rem(mem, 2)
    z = lax.rem(lax.div(mem, 2), NZ)
    x_hi = lax.div(mem, 2 * NZ)
    y = lax.div(hist, 2)
    x_lo = lax.rem(hist, 2)
    chip = mem - core
    y_next = (lax.rem(y + 1, NY), lax.rem(y + NY - 1, NY))
    y_far = lax.rem(y + 2, NY)
    z_next = (lax.rem(z + 1, NZ), lax.rem(z + NZ - 1, NZ))

    def at_mem(xx, zz, q):
        return xx * (2 * NZ) + zz * 2 + q

    def at_hist(yy, xx):
        return yy * 2 + xx

    def send(src, dst, send_sem, recv_sem, where):
        return pltpu.make_async_remote_copy(
            src_ref=src, dst_ref=dst, send_sem=send_sem, recv_sem=recv_sem, device_id=where, device_id_type=MESH
        )

    other_core = (chip + 1 - core, hist)
    other_x = at_hist(y, 1 - x_lo)
    peers = [other_core]
    peers += [(chip + q, other_x) for q in range(2)]
    peers += [(chip + q, at_hist(yy, x_lo)) for yy in (*y_next, y_far) for q in range(2)]
    waits = len(peers) + 1 + 8
    peers += [(at_mem(1 - x_hi, z, core), hist)]
    for way in range(2):
        for part in PARTS[way]:
            source = lax.rem(z + (part[1], NZ - part[1])[way], NZ)
            peers += [(at_mem(xx, source, way), hist) for xx in range(2)]
    barrier = pltpu.get_barrier_semaphore()
    for peer in peers:
        pl.semaphore_signal(barrier, inc=1, device_id=peer, device_id_type=MESH)

    loads = [
        pltpu.make_async_copy(src, dst, load_sem.at[n])
        for n, (src, dst) in enumerate((
            (coupling_hbm, coupling_ref), (memory_hbm, memory_ref), (time_hbm, time_deal), (column_hbm, column_times),
            (window_hbm, window_start), (hamiltonian_hbm, hamiltonian_ref), (panel_hbm, panel_ref),
            (block_ref, blocks.at[core]),
        ))
    ]
    for copy in loads:
        copy.start()

    loads[0].wait()
    coupling_high, coupling_low = halves(coupling_ref[...])
    left_high, left_low = pair_form(coupling_high), pair_form(coupling_low)
    left = jnp.concatenate([left_high, left_high, left_low], axis=1)
    right_high, right_low = lane_form(coupling_high), lane_form(coupling_low)
    right = jnp.concatenate([right_high, right_high, right_low], axis=0)
    loads[1].wait()
    for u, tile in enumerate(sigma_of(memory_ref[...], left, right)):
        own_sigma[u % 2, u // 2] = tile.astype(BF16)

    pl.semaphore_wait(barrier, waits)

    mine = core * NY + y
    early = lax.div(lax.rem(2 * x_lo + 2 * NZ + 3 - z, 4), 2)
    first = []
    for n in range(2):
        u = early if n == 0 else 1 - early
        here = old_sigma.at[2 * x_lo + u, mine]
        arrival = tile_sem.at[2 * x_lo + u, mine]
        targets = []
        for yy in (y_far, *y_next):
            targets += [(q, (chip + q, at_hist(yy, x_lo))) for q in range(2)]
        targets += [(q, (chip + q, other_x)) for q in range(2)]
        targets += [(1 - core, other_core)]
        for i, (q, where) in enumerate(targets):
            copy = send(own_sigma.at[q, u], here, first_send.at[n, i], arrival, where)
            copy.start()
            first.append(copy)
        pltpu.make_async_copy(own_sigma.at[core, u], here, arrival).start()
    block_there = send(block_ref, blocks.at[core], block_send, block_sem, other_core)
    block_there.start()

    def arrived(dst, sem):
        send(dst, dst, sem, sem, other_core).wait_recv()

    sign = jnp.where(lax.broadcasted_iota(jnp.int32, (64, 128), 1) < 64, -1.0, 1.0)
    for n in (2, 3, 4):
        loads[n].wait()
    start = window_start[0]

    def build(which):
        for k in range(4):
            slot_time = time_deal[(chip + which) * 4 + k]
            for j in range(8):
                keep = (slot_time >= column_times[hist * 8 + j]) & (slot_time >= start)
                level = jnp.where(keep, 1.0, 0.0)
                tile = blocks[which, k, j].astype(F32) * level
                row = pl.multiple_of((which * 4 + k) * 128, 128)
                forms[pl.ds(row, 64), j * 128 : (j + 1) * 128] = tile.astype(BF16)
                forms[pl.ds(row + 64, 64), j * 128 : (j + 1) * 128] = (pltpu.roll(tile, 64, 1) * sign).astype(BF16)

    loads[7].wait()
    build(core)

    loads[5].wait()
    loads[6].wait()
    panel = panel_ref[...]
    applied = dot(pair_form(hamiltonian_ref[...]), panel)
    turned = pltpu.roll(applied, 64, 1) * jnp.where(lax.broadcasted_iota(jnp.int32, (128, 128), 1) < 64, 1.0, -1.0)
    base = panel.astype(F32) + TIME_STEP * turned

    def time_of(n):
        return lax.rem(z + ORDER[n], 4)

    def tile_in(t, kk):
        arrived(old_sigma.at[t, kk], tile_sem.at[t, kk])

    def pass_on(n):
        t = time_of(n)
        inside = lax.div(t, 2) == x_lo

        @pl.when(inside)
        def _():
            for q in range(2):
                kk = q * NY + y_far
                tile_in(t, kk)
                send(old_sigma.at[t, kk], old_sigma.at[t, kk], pass_send.at[t, q], tile_sem.at[t, kk], (mem, other_x)).start()

        @pl.when(jnp.logical_not(inside))
        def _():
            for q in range(2):
                kk = q * NY + y
                tile_in(t, kk)
                for d in range(2):
                    send(old_sigma.at[t, kk], old_sigma.at[t, kk], pass_send.at[t, 2 * q + d], tile_sem.at[t, kk],
                         (mem, at_hist(y_next[d], x_lo))).start()

    def complete(n):
        t = time_of(n)
        rest = jnp.where(lax.div(t, 2) == x_lo, y, y_far)
        for q in range(2):
            tile_in(t, q * NY + rest)
            for yy in y_next:
                tile_in(t, q * NY + yy)

    def multiply(n):
        t = time_of(n)
        lhs = jnp.concatenate([old_sigma[t, kk] for kk in range(8)], axis=1)
        for j in range(4):
            product = dot(lhs, forms[:, j * 256 : (j + 1) * 256])
            for i in range(2):
                value = product[:, i * 128 : (i + 1) * 128]
                partial[t, (2 * j + i) % 4, (2 * j + i) // 4] = value
                shared_out[t, (2 * j + i) % 4, (2 * j + i) // 4] = value.astype(BF16)

    def drain_passes(n):
        t = time_of(n)
        inside = lax.div(t, 2) == x_lo
        for i in range(2):
            send(old_sigma.at[t, i], old_sigma.at[t, i], pass_send.at[t, i], pass_send.at[t, i], other_core).wait_send()

        @pl.when(jnp.logical_not(inside))
        def _():
            for i in range(2, 4):
                send(old_sigma.at[t, i], old_sigma.at[t, i], pass_send.at[t, i], pass_send.at[t, i], other_core).wait_send()

    def spot(way, n):
        far = lax.rem(z + (NZ - n, n)[way], NZ)
        return lax.rem(far, 4), lax.div(far, 4)

    def term(xx):
        t, column = spot(1, 0)
        return partial[t, column, xx]

    def share(order):
        for way in range(2):

            @pl.when(core == 1 - way)
            def _():
                for n in range(1, (BEHIND, AHEAD)[way] + 1):
                    if (n if way else -n) % 4 == ORDER[order]:
                        t, column = spot(way, n)
                        send(shared_out.at[t, column], shared_in.at[n - 1], shared_send.at[n - 1], shared_sem.at[n - 1],
                             other_core).start()

    def drain_share(n):
        here = shared_in.at[n - 1]
        send(here, here, shared_send.at[n - 1], shared_send.at[n - 1], other_core).wait_send()

    def chain(way, s):
        for part, (top, end) in enumerate(PARTS[way]):
            n = top - s
            if n < end:
                continue
            t, column = spot(way, n)
            beyond = lax.rem(z + (NZ - end, end)[way], NZ)
            for i in range(2):
                q = (core, 1 - core)[i]
                if i == 1:
                    arrived(shared_in.at[n - 1], shared_sem.at[n - 1])
                for b in range(2):
                    value = partial[t, column, b] if i == 0 else shared_in[n - 1, b].astype(F32)
                    if s > 0:
                        arrived(chain_in.at[n - 1, i, b], chain_sem.at[n - 1, i, b])
                        value = value + chain_in[n - 1, i, b].astype(F32)
                    chain_out[n - 1, i, b] = value.astype(BF16)
                    if n > end:
                        dst, sem = chain_in.at[n - 2, i, b], chain_sem.at[n - 2, i, b]
                        where = (at_mem(x_hi, z_next[1 - way], core), hist)
                    else:
                        slot = 4 * way + 2 * part + x_hi
                        dst, sem, where = last_in.at[slot], last_sem.at[slot], (at_mem(b, beyond, q), hist)
                    send(chain_out.at[n - 1, i, b], dst, chain_send.at[n - 1, i, b], sem, where).start()

    def drain_chain(n):
        for i in range(2):
            for b in range(2):
                here = chain_out.at[n - 1, i, b]
                send(here, here, chain_send.at[n - 1, i, b], chain_send.at[n - 1, i, b], other_core).wait_send()

    def step(n):
        complete(n)
        multiply(n)
        share(n)

    pass_on(0)
    pass_on(1)
    block_there.wait_recv()
    build(1 - core)
    pass_on(2)
    pass_on(3)
    step(0)
    pl.when(core == 0)(lambda: chain(0, 0))
    step(1)
    cross_out[...] = term(1 - x_hi).astype(BF16)
    cross = send(cross_out, last_in.at[8], cross_send, last_sem.at[8], (at_mem(1 - x_hi, z, core), hist))
    cross.start()
    pl.when(core == 1)(lambda: chain(1, 0))
    step(2)
    pl.when(core == 0)(lambda: chain(0, 1))
    step(3)

    @pl.when(core == 1)
    def _():
        for s in range(1, 4):
            chain(1, s)
        for n in range(1, BEHIND + 1):
            drain_share(n)
        for n in (8, 7, 4, 3):
            drain_chain(n)

    @pl.when(core == 0)
    def _():
        for s in range(2, 4):
            chain(0, s)
        for n in range(1, AHEAD + 1):
            drain_share(n)
        for n in (7, 6, 3, 2):
            drain_chain(n)

    for copy in first + [block_there]:
        copy.wait_send()
    for n in range(4):
        drain_passes(n)

    total = term(x_hi)
    for n in (8, 2, 3, 6, 7, 0, 1, 4, 5):
        arrived(last_in.at[n], last_sem.at[n])
        total = total + last_in[n].astype(F32)
    advanced = (base + TIME_STEP * total).astype(BF16)
    both_ref[0] = advanced
    [new_sigma] = sigma_of(advanced, left, right)
    both_ref[1] = new_sigma.astype(BF16)

    cross.wait_send()

    @pl.when(core == 0)
    def _():
        for n in (5, 4, 1):
            drain_chain(n)

    @pl.when(core == 1)
    def _():
        for n in (6, 5, 2, 1):
            drain_chain(n)


def local(memory_block, memory_rows, panel_rows, time_deal, column_times, window_start, coupling, hamiltonian):
    tile = (128, 128)
    dma = pltpu.SemaphoreType.DMA
    vmem = pl.BlockSpec(memory_space=pltpu.VMEM)
    hbm = pl.BlockSpec(memory_space=pltpu.HBM)
    both = pl.pallas_call(
        kernel,
        out_shape=jax.ShapeDtypeStruct((2, *tile), BF16),
        in_specs=[hbm] * 8,
        out_specs=vmem,
        scratch_shapes=[
            pltpu.SMEM(time_deal.shape, jnp.int32),
            pltpu.SMEM(column_times.shape, jnp.int32),
            pltpu.SMEM(window_start.shape, jnp.int32),
            pltpu.VMEM((512, 128), BF16),
            pltpu.VMEM(tile, BF16),
            pltpu.VMEM(coupling.shape, F32),
            pltpu.VMEM(hamiltonian.shape, BF16),
            pltpu.VMEM((2, 4, 8, 64, 128), BF16),
            pltpu.VMEM((1024, 1024), BF16),
            pltpu.VMEM((2, 2, *tile), BF16),
            pltpu.VMEM((4, 8, *tile), BF16),
            pltpu.VMEM((4, 4, 2, *tile), F32),
            pltpu.VMEM((4, 4, 2, *tile), BF16),
            pltpu.VMEM((AHEAD, 2, *tile), BF16),
            pltpu.VMEM((AHEAD - 1, 2, 2, *tile), BF16),
            pltpu.VMEM((AHEAD, 2, 2, *tile), BF16),
            pltpu.VMEM((9, *tile), BF16),
            pltpu.VMEM(tile, BF16),
            dma((8,)), dma, dma, dma((4, 8)), dma((2, 9)), dma((4, 4)),
            dma((AHEAD,)), dma((AHEAD,)), dma((AHEAD - 1, 2, 2)), dma((AHEAD, 2, 2)), dma((9,)), dma,
        ],
        compiler_params=pltpu.CompilerParams(
            collective_id=0, has_side_effects=True, vmem_limit_bytes=60 * 2**20
        ),
        cost_estimate=pl.CostEstimate(flops=1100000000, bytes_accessed=2000000, transcendentals=0),
    )(
        time_deal, column_times, window_start, memory_block,
        memory_rows.reshape(512, 128), panel_rows.reshape(128, 128), coupling, hamiltonian,
    )
    return both[0].reshape(panel_rows.shape), both[1].reshape(panel_rows.shape)


def solution(mesh):
    in_specs = (
        P("mem", "hist", None, None),
        P(("mem", "hist"), None, None),
        P(("hist", "mem"), None, None),
        P(),
        P(),
        P(),
        P(),
        P(),
    )
    out_specs = (P(("hist", "mem"), None, None), P(("hist", "mem"), None, None))
    return jax.shard_map(local, mesh=mesh, in_specs=in_specs, out_specs=out_specs, check_vma=False)
```

```python
import jax
import jax.numpy as jnp
from jax import lax
from jax.experimental import pallas as pl
from jax.experimental.pallas import tpu as pltpu
from jax.sharding import PartitionSpec as P


MESH = pl.DeviceIdType.MESH
BF16 = jnp.bfloat16
F32 = jnp.float32
P_SIZE = 8
TIME_STEP = 0.02
NZ = 16
NY = 4
AHEAD, BEHIND = 8, 7
PARTS = (((7, 4), (3, 1)), ((8, 5), (4, 1)))
ORDER = (1, 0, 2, 3)


def halves(x):
    high = x.astype(BF16)
    return high, (x - high.astype(F32)).astype(BF16)


def dot(a, b):
    return jnp.dot(a, b, preferred_element_type=F32)


def chosen(shape, test):
    rows = lax.broadcasted_iota(jnp.int32, shape, 0)
    columns = lax.broadcasted_iota(jnp.int32, shape, 1)
    return jnp.where(test(rows, columns), 1.0, 0.0).astype(BF16)


def pair_form(small):
    spread = chosen((128, 64), lambda r, c: (r >> 1) == c)
    gather = chosen((64, 128), lambda r, c: r == (c >> 1))
    wide = dot(dot(spread, small).astype(BF16), gather)
    same = chosen((128, 128), lambda r, c: (r & 1) == (c & 1))
    return wide.astype(BF16) * same


def lane_form(small):
    spread = chosen((128, 64), lambda r, c: (r & 63) == c)
    gather = chosen((64, 128), lambda r, c: r == (c & 63))
    turned = lax.dot_general(spread, small, (((1,), (1,)), ((), ())), preferred_element_type=F32)
    return dot(turned.astype(BF16), gather).astype(BF16)


def sigma_of(x, left, right):
    count = x.shape[0] // 128
    wide = x.astype(F32)
    high, low = halves(wide * wide)
    over = dot(jnp.concatenate([high, low, high], axis=1), right)
    high, low = halves(over)
    result = []
    for n in range(count):
        rows = slice(n * 128, (n + 1) * 128)
        stacked = jnp.concatenate([high[rows], low[rows], high[rows]], axis=0)
        result.append(-(wide[rows] * dot(left, stacked)))
    return result


def kernel(
    time_hbm, column_hbm, window_hbm, block_ref, memory_hbm, panel_hbm, coupling_hbm, hamiltonian_hbm,
    both_ref,
    time_deal, column_times, window_start, memory_ref, panel_ref, coupling_ref, hamiltonian_ref,
    blocks, forms, own_sigma, old_sigma, partial, shared_out, shared_in, chain_in, chain_out, last_in, cross_out,
    load_sem, block_sem, block_send, tile_sem, first_send, pass_send,
    shared_send, shared_sem, chain_sem, chain_send, last_sem, cross_send,
):
    mem = lax.axis_index("mem")
    hist = lax.axis_index("hist")
    core = lax.rem(mem, 2)
    z = lax.rem(lax.div(mem, 2), NZ)
    x_hi = lax.div(mem, 2 * NZ)
    y = lax.div(hist, 2)
    x_lo = lax.rem(hist, 2)
    chip = mem - core
    y_next = (lax.rem(y + 1, NY), lax.rem(y + NY - 1, NY))
    y_far = lax.rem(y + 2, NY)
    z_next = (lax.rem(z + 1, NZ), lax.rem(z + NZ - 1, NZ))

    def at_mem(xx, zz, q):
        return xx * (2 * NZ) + zz * 2 + q

    def at_hist(yy, xx):
        return yy * 2 + xx

    def send(src, dst, send_sem, recv_sem, where):
        return pltpu.make_async_remote_copy(
            src_ref=src, dst_ref=dst, send_sem=send_sem, recv_sem=recv_sem, device_id=where, device_id_type=MESH
        )

    other_core = (chip + 1 - core, hist)
    other_x = at_hist(y, 1 - x_lo)
    peers = [other_core]
    peers += [(chip + q, other_x) for q in range(2)]
    peers += [(chip + q, at_hist(yy, x_lo)) for yy in (*y_next, y_far) for q in range(2)]
    waits = len(peers) + 1 + 8
    peers += [(at_mem(1 - x_hi, z, core), hist)]
    for way in range(2):
        for part in PARTS[way]:
            source = lax.rem(z + (part[1], NZ - part[1])[way], NZ)
            peers += [(at_mem(xx, source, way), hist) for xx in range(2)]
    barrier = pltpu.get_barrier_semaphore()
    for peer in peers:
        pl.semaphore_signal(barrier, inc=1, device_id=peer, device_id_type=MESH)

    loads = [
        pltpu.make_async_copy(src, dst, load_sem.at[n])
        for n, (src, dst) in enumerate((
            (coupling_hbm, coupling_ref), (memory_hbm, memory_ref), (time_hbm, time_deal), (column_hbm, column_times),
            (window_hbm, window_start), (hamiltonian_hbm, hamiltonian_ref), (panel_hbm, panel_ref),
            (block_ref, blocks.at[core]),
        ))
    ]
    for copy in loads:
        copy.start()

    loads[0].wait()
    coupling_high, coupling_low = halves(coupling_ref[...])
    left_high, left_low = pair_form(coupling_high), pair_form(coupling_low)
    left = jnp.concatenate([left_high, left_high, left_low], axis=1)
    right_high, right_low = lane_form(coupling_high), lane_form(coupling_low)
    right = jnp.concatenate([right_high, right_high, right_low], axis=0)
    loads[1].wait()
    for u, tile in enumerate(sigma_of(memory_ref[...], left, right)):
        own_sigma[u % 2, u // 2] = tile.astype(BF16)

    pl.semaphore_wait(barrier, waits)

    mine = core * NY + y
    early = lax.div(lax.rem(2 * x_lo + 2 * NZ + 3 - z, 4), 2)
    first = []
    for n in range(2):
        u = early if n == 0 else 1 - early
        here = old_sigma.at[2 * x_lo + u, mine]
        arrival = tile_sem.at[2 * x_lo + u, mine]
        targets = []
        for yy in (y_far, *y_next):
            targets += [(q, (chip + q, at_hist(yy, x_lo))) for q in range(2)]
        targets += [(q, (chip + q, other_x)) for q in range(2)]
        targets += [(1 - core, other_core)]
        for i, (q, where) in enumerate(targets):
            copy = send(own_sigma.at[q, u], here, first_send.at[n, i], arrival, where)
            copy.start()
            first.append(copy)
        pltpu.make_async_copy(own_sigma.at[core, u], here, arrival).start()
    block_there = send(block_ref, blocks.at[core], block_send, block_sem, other_core)
    block_there.start()

    def arrived(dst, sem):
        send(dst, dst, sem, sem, other_core).wait_recv()

    sign = jnp.where(lax.broadcasted_iota(jnp.int32, (64, 128), 1) < 64, -1.0, 1.0)
    for n in (2, 3, 4):
        loads[n].wait()
    start = window_start[0]

    def build(which):
        for k in range(4):
            slot_time = time_deal[(chip + which) * 4 + k]
            for j in range(8):
                keep = (slot_time >= column_times[hist * 8 + j]) & (slot_time >= start)
                level = jnp.where(keep, 1.0, 0.0)
                tile = blocks[which, k, j].astype(F32) * level
                row = pl.multiple_of((which * 4 + k) * 128, 128)
                forms[pl.ds(row, 64), j * 128 : (j + 1) * 128] = tile.astype(BF16)
                forms[pl.ds(row + 64, 64), j * 128 : (j + 1) * 128] = (pltpu.roll(tile, 64, 1) * sign).astype(BF16)

    loads[7].wait()
    build(core)

    loads[5].wait()
    loads[6].wait()
    panel = panel_ref[...]
    applied = dot(pair_form(hamiltonian_ref[...]), panel)
    turned = pltpu.roll(applied, 64, 1) * jnp.where(lax.broadcasted_iota(jnp.int32, (128, 128), 1) < 64, 1.0, -1.0)
    base = panel.astype(F32) + TIME_STEP * turned

    def time_of(n):
        return lax.rem(z + ORDER[n], 4)

    def tile_in(t, kk):
        arrived(old_sigma.at[t, kk], tile_sem.at[t, kk])

    def pass_on(n):
        t = time_of(n)
        inside = lax.div(t, 2) == x_lo

        @pl.when(inside)
        def _():
            for q in range(2):
                kk = q * NY + y_far
                tile_in(t, kk)
                send(old_sigma.at[t, kk], old_sigma.at[t, kk], pass_send.at[t, q], tile_sem.at[t, kk], (mem, other_x)).start()

        @pl.when(jnp.logical_not(inside))
        def _():
            for q in range(2):
                kk = q * NY + y
                tile_in(t, kk)
                for d in range(2):
                    send(old_sigma.at[t, kk], old_sigma.at[t, kk], pass_send.at[t, 2 * q + d], tile_sem.at[t, kk],
                         (mem, at_hist(y_next[d], x_lo))).start()

    def complete(n):
        t = time_of(n)
        rest = jnp.where(lax.div(t, 2) == x_lo, y, y_far)
        for q in range(2):
            tile_in(t, q * NY + rest)
            for yy in y_next:
                tile_in(t, q * NY + yy)

    def multiply(n):
        t = time_of(n)
        lhs = jnp.concatenate([old_sigma[t, kk] for kk in range(8)], axis=1)
        for j in range(4):
            product = dot(lhs, forms[:, j * 256 : (j + 1) * 256])
            for i in range(2):
                value = product[:, i * 128 : (i + 1) * 128]
                partial[t, (2 * j + i) % 4, (2 * j + i) // 4] = value
                shared_out[t, (2 * j + i) % 4, (2 * j + i) // 4] = value.astype(BF16)

    def drain_passes(n):
        t = time_of(n)
        inside = lax.div(t, 2) == x_lo
        for i in range(2):
            send(old_sigma.at[t, i], old_sigma.at[t, i], pass_send.at[t, i], pass_send.at[t, i], other_core).wait_send()

        @pl.when(jnp.logical_not(inside))
        def _():
            for i in range(2, 4):
                send(old_sigma.at[t, i], old_sigma.at[t, i], pass_send.at[t, i], pass_send.at[t, i], other_core).wait_send()

    def spot(way, n):
        far = lax.rem(z + (NZ - n, n)[way], NZ)
        return lax.rem(far, 4), lax.div(far, 4)

    def term(xx):
        t, column = spot(1, 0)
        return partial[t, column, xx]

    def share(order):
        for way in range(2):

            @pl.when(core == 1 - way)
            def _():
                for n in range(1, (BEHIND, AHEAD)[way] + 1):
                    if (n if way else -n) % 4 == ORDER[order]:
                        t, column = spot(way, n)
                        send(shared_out.at[t, column], shared_in.at[n - 1], shared_send.at[n - 1], shared_sem.at[n - 1],
                             other_core).start()

    def drain_share(n):
        here = shared_in.at[n - 1]
        send(here, here, shared_send.at[n - 1], shared_send.at[n - 1], other_core).wait_send()

    def chain(way, s):
        for part, (top, end) in enumerate(PARTS[way]):
            n = top - s
            if n < end:
                continue
            t, column = spot(way, n)
            beyond = lax.rem(z + (NZ - end, end)[way], NZ)
            for i in range(2):
                q = (core, 1 - core)[i]
                if i == 1:
                    arrived(shared_in.at[n - 1], shared_sem.at[n - 1])
                for b in range(2):
                    value = partial[t, column, b] if i == 0 else shared_in[n - 1, b].astype(F32)
                    if s > 0:
                        arrived(chain_in.at[n - 1, i, b], chain_sem.at[n - 1, i, b])
                        value = value + chain_in[n - 1, i, b].astype(F32)
                    chain_out[n - 1, i, b] = value.astype(BF16)
                    if n > end:
                        dst, sem = chain_in.at[n - 2, i, b], chain_sem.at[n - 2, i, b]
                        where = (at_mem(x_hi, z_next[1 - way], core), hist)
                    else:
                        slot = 4 * way + 2 * part + x_hi
                        dst, sem, where = last_in.at[slot], last_sem.at[slot], (at_mem(b, beyond, q), hist)
                    send(chain_out.at[n - 1, i, b], dst, chain_send.at[n - 1, i, b], sem, where).start()

    def drain_chain(n):
        for i in range(2):
            for b in range(2):
                here = chain_out.at[n - 1, i, b]
                send(here, here, chain_send.at[n - 1, i, b], chain_send.at[n - 1, i, b], other_core).wait_send()

    def step(n):
        complete(n)
        multiply(n)
        share(n)

    pass_on(0)
    pass_on(1)
    block_there.wait_recv()
    build(1 - core)
    pass_on(2)
    pass_on(3)
    step(0)
    step(1)
    cross_out[...] = term(1 - x_hi).astype(BF16)
    cross = send(cross_out, last_in.at[8], cross_send, last_sem.at[8], (at_mem(1 - x_hi, z, core), hist))
    cross.start()
    pl.when(core == 0)(lambda: chain(0, 0))
    step(2)
    pl.when(core == 1)(lambda: chain(1, 0))
    step(3)
    pl.when(core == 0)(lambda: chain(0, 1))

    @pl.when(core == 1)
    def _():
        for s in range(1, 4):
            chain(1, s)
        for n in range(1, BEHIND + 1):
            drain_share(n)
        for n in (8, 7, 4, 3):
            drain_chain(n)

    @pl.when(core == 0)
    def _():
        for s in range(2, 4):
            chain(0, s)
        for n in range(1, AHEAD + 1):
            drain_share(n)
        for n in (7, 6, 3, 2):
            drain_chain(n)

    for copy in first + [block_there]:
        copy.wait_send()
    for n in range(4):
        drain_passes(n)

    total = term(x_hi)
    for n in (8, 2, 3, 6, 7, 0, 1, 4, 5):
        arrived(last_in.at[n], last_sem.at[n])
        total = total + last_in[n].astype(F32)
    advanced = (base + TIME_STEP * total).astype(BF16)
    both_ref[0] = advanced
    [new_sigma] = sigma_of(advanced, left, right)
    both_ref[1] = new_sigma.astype(BF16)

    cross.wait_send()

    @pl.when(core == 0)
    def _():
        for n in (5, 4, 1):
            drain_chain(n)

    @pl.when(core == 1)
    def _():
        for n in (6, 5, 2, 1):
            drain_chain(n)


def local(memory_block, memory_rows, panel_rows, time_deal, column_times, window_start, coupling, hamiltonian):
    tile = (128, 128)
    dma = pltpu.SemaphoreType.DMA
    vmem = pl.BlockSpec(memory_space=pltpu.VMEM)
    hbm = pl.BlockSpec(memory_space=pltpu.HBM)
    both = pl.pallas_call(
        kernel,
        out_shape=jax.ShapeDtypeStruct((2, *tile), BF16),
        in_specs=[hbm] * 8,
        out_specs=vmem,
        scratch_shapes=[
            pltpu.SMEM(time_deal.shape, jnp.int32),
            pltpu.SMEM(column_times.shape, jnp.int32),
            pltpu.SMEM(window_start.shape, jnp.int32),
            pltpu.VMEM((512, 128), BF16),
            pltpu.VMEM(tile, BF16),
            pltpu.VMEM(coupling.shape, F32),
            pltpu.VMEM(hamiltonian.shape, BF16),
            pltpu.VMEM((2, 4, 8, 64, 128), BF16),
            pltpu.VMEM((1024, 1024), BF16),
            pltpu.VMEM((2, 2, *tile), BF16),
            pltpu.VMEM((4, 8, *tile), BF16),
            pltpu.VMEM((4, 4, 2, *tile), F32),
            pltpu.VMEM((4, 4, 2, *tile), BF16),
            pltpu.VMEM((AHEAD, 2, *tile), BF16),
            pltpu.VMEM((AHEAD - 1, 2, 2, *tile), BF16),
            pltpu.VMEM((AHEAD, 2, 2, *tile), BF16),
            pltpu.VMEM((9, *tile), BF16),
            pltpu.VMEM(tile, BF16),
            dma((8,)), dma, dma, dma((4, 8)), dma((2, 9)), dma((4, 4)),
            dma((AHEAD,)), dma((AHEAD,)), dma((AHEAD - 1, 2, 2)), dma((AHEAD, 2, 2)), dma((9,)), dma,
        ],
        compiler_params=pltpu.CompilerParams(
            collective_id=0, has_side_effects=True, vmem_limit_bytes=60 * 2**20
        ),
        cost_estimate=pl.CostEstimate(flops=1100000000, bytes_accessed=2000000, transcendentals=0),
    )(
        time_deal, column_times, window_start, memory_block,
        memory_rows.reshape(512, 128), panel_rows.reshape(128, 128), coupling, hamiltonian,
    )
    return both[0].reshape(panel_rows.shape), both[1].reshape(panel_rows.shape)


def solution(mesh):
    in_specs = (
        P("mem", "hist", None, None),
        P(("mem", "hist"), None, None),
        P(("hist", "mem"), None, None),
        P(),
        P(),
        P(),
        P(),
        P(),
    )
    out_specs = (P(("hist", "mem"), None, None), P(("hist", "mem"), None, None))
    return jax.shard_map(local, mesh=mesh, in_specs=in_specs, out_specs=out_specs, check_vma=False)
```
